32 devices in a mesh: groups: 2 (over y), lat: 4 (over z), width: 4 (over x, core).
Axes of the slice: x: 2, y: 2, z: 4, core: 2. Of those that a mesh axis runs over, the one named last changes fastest.
Arguments:
- activations: bfloat16 [1024, 4096], P(('groups', 'lat'), 'width'), parts along dimension 0, may hold values from -6 to 6
- rest_recon: bfloat16 [1024, 4096], P(('groups', 'lat'), 'width'), parts along dimension 0, may hold values from -6 to 6
- w_enc: bfloat16 [4096, 768], P('width', 'lat'), may hold values from -0.09375 to 0.09375
- b_enc: float32 [768], P('lat'), may hold values from -3 to 3
- w_dec: bfloat16 [768, 4096], P('lat', 'width'), may hold values from -0.21875 to 0.21875
- b_dec: float32 [4096], P('width'), may hold values from -3 to 3
Outputs:
- grad_enc: float32 [8192, 768], P(('groups', 'width'), 'lat'), parts along dimension 0
- grad_benc: float32 [1536], P(('groups', 'lat')), parts along dimension 0
- grad_dec: float32 [1536, 4096], P(('groups', 'lat'), 'width'), parts along dimension 0
- grad_bdec: float32 [8192], P(('groups', 'width')), parts along dimension 0
The draws below stay inside these ranges and needn't reach their ends.
There are 2 independent parts, one for each index of `groups`. The reference program is written for one: setup_inputs(seed, part) draws one part's arguments, and reference() takes and returns one part's arrays. A program takes and returns all parts, laid end to end along the dimension named above; an argument that names none is the same for every part. Nothing has to cross between parts.
All inputs are finite; a program needn't handle non-finite values.
Results may differ from the reference program's by a relative error of at most 0.012.
Values may be sent and summed in bfloat16 or wider, within the bound.
No kernel may reach another device: no remote copies, remote signals or barrier semaphores. Data moves between devices by JAX's collectives and lax.ppermute only.
A program may use at most 64 MiB of HBM per device.

```python
import jax
import jax.numpy as jnp
from jax import lax

D = 4096
LAT_DEV = 192
LAT = 768
ROWS = 512
N_LAT = 4
N_WIDTH = 4


def block_scale(own_key, shape, cuts, smallest, top_value):
    def one(dim, shards_of):
        steps = jax.random.uniform(jax.random.fold_in(jax.random.fold_in(own_key, 6), dim), (shards_of,), jnp.float32, smallest / len(cuts), top_value / len(cuts))
        return jnp.repeat(jnp.exp(steps), shape[dim] // shards_of).reshape((-1,) + (1,) * (len(shape) - dim - 1))

    gain = one(*cuts[0])
    for cut in cuts[1:]:
        gain = gain * one(*cut)
    return gain


def normal_values(rng, dims, width, bound, pieces=(), kind=jnp.bfloat16):
    loudness = block_scale(rng, dims, pieces, -0.22, 0.18) if pieces else 1.0
    array = jax.random.normal(rng, dims, jnp.float32) * width * loudness
    return jnp.minimum(jnp.maximum(array, -bound), bound).astype(kind)


def setup_inputs(seed: int = 0, part: int = 0) -> dict:
    keys = jax.random.split(jax.random.key(seed), 7)
    part_splits = jax.random.split(jax.random.fold_in(keys[6], part), 7)
    return {
        "activations": normal_values(part_splits[0], (ROWS, D), 1.0, 6.0, ((0, 4), (1, 4))),
        "rest_recon": normal_values(part_splits[1], (ROWS, D), 0.5, 6.0, ((0, 4), (1, 4))),
        "w_enc": normal_values(keys[2], (D, LAT), D ** -0.5, 0.09375, ((0, 4), (1, 4))),
        "b_enc": normal_values(keys[3], (LAT,), 0.3, 3.0, ((0, 4),), jnp.float32),
        "w_dec": normal_values(keys[4], (LAT, D), LAT ** -0.5, 0.21875, ((0, 4), (1, 4))),
        "b_dec": normal_values(keys[5], (D,), 0.5, 3.0, ((0, 4),), jnp.float32),
    }


sparsity_coef = 3.0

def reference(activations, rest_recon, w_enc, b_enc, w_dec, b_dec):
    row_scale = 1.0 / jnp.sqrt(jnp.float32(ROWS))
    cols = D // N_WIDTH
    centered = (activations.astype(jnp.float32) - b_dec).astype(jnp.bfloat16)
    pre = jnp.zeros((ROWS, LAT), jnp.float32)
    for block in range(N_WIDTH):
        lo = block * cols
        term = jnp.dot(centered[:, lo:lo + cols], w_enc[lo:lo + cols, :], preferred_element_type=jnp.float32)
        pre = pre + term.astype(jnp.bfloat16).astype(jnp.float32)
    pre = pre + b_enc
    codes = jnp.maximum(pre, 0.0).astype(jnp.bfloat16)
    dec_float = w_dec.astype(jnp.float32)
    norms = jnp.sqrt(lax.optimization_barrier(jnp.sum(dec_float * dec_float, axis=1)) + 1e-06)
    recon = jnp.zeros((ROWS, D), jnp.float32)
    for block in range(N_LAT):
        lo = block * LAT_DEV
        term = jnp.dot(codes[:, lo:lo + LAT_DEV], w_dec[lo:lo + LAT_DEV, :], preferred_element_type=jnp.float32)
        recon = recon + term.astype(jnp.bfloat16).astype(jnp.float32)
    error_rows = rest_recon.astype(jnp.float32) + recon + b_dec - activations.astype(jnp.float32)
    res_grad = (2.0 * row_scale * error_rows).astype(jnp.bfloat16)
    code_sum = jnp.zeros((ROWS, LAT), jnp.float32)
    for block in range(N_WIDTH):
        lo = block * cols
        term = jnp.dot(res_grad[:, lo:lo + cols], w_dec[:, lo:lo + cols].T, preferred_element_type=jnp.float32)
        code_sum = code_sum + term.astype(jnp.bfloat16).astype(jnp.float32)
    pre_grad = jnp.where(codes > 0, code_sum + sparsity_coef * row_scale * norms, 0.0).astype(jnp.bfloat16)
    grad_enc = jnp.dot(centered.T, pre_grad, preferred_element_type=jnp.float32)
    grad_benc = lax.optimization_barrier(jnp.sum(pre_grad.astype(jnp.float32), axis=0))
    code_total = lax.optimization_barrier(jnp.sum(codes.astype(jnp.float32), axis=0))
    grad_dec = jnp.dot(codes.T, res_grad, preferred_element_type=jnp.float32)
    grad_dec = grad_dec + (sparsity_coef * row_scale * code_total / norms)[:, None] * dec_float
    enc_term = jnp.dot(w_enc.astype(jnp.float32), grad_benc, precision=lax.Precision.HIGHEST)
    grad_bdec = lax.optimization_barrier(jnp.sum(res_grad.astype(jnp.float32), axis=0)) - enc_term
    return (grad_enc, grad_benc, grad_dec, grad_bdec)
```

```python
import jax
import jax.numpy as jnp
from jax import lax
from jax.sharding import PartitionSpec as P

sparsity_coef = 3.0
f32 = jnp.float32
bf16 = jnp.bfloat16


def swap(value, axis, distance):
    count = lax.axis_size(axis)
    return lax.ppermute(value, axis, [(i, i ^ distance) for i in range(count)])


def after(value, *earlier):
    return lax.optimization_barrier((value, *earlier))[0]


def lat_gather(block):
    count = lax.axis_size("lat")
    if count != 4:
        return [block] + [swap(block, "lat", k) for k in range(1, count)]
    z = lax.axis_index("lat")
    inner = (z == 1) | (z == 2)
    near = swap(block, "lat", 1)
    middle = lax.ppermute(block, "lat", [(1, 2), (2, 1)])
    out = lax.ppermute(middle, "lat", [(1, 0), (2, 3)])
    across = lax.ppermute(near, "lat", [(1, 2), (2, 1)])
    two = jnp.where(inner, across, out)
    ends = lax.ppermute(across, "lat", [(1, 0), (2, 3)])
    three = jnp.where(inner, middle, ends)
    return [block, near, two, three]


def width_sum(part):
    count = lax.axis_size("width")
    own = part.astype(bf16)
    if count == 4:
        others = [swap(own, "width", k) for k in (1, 2, 3)]
        return (own.astype(f32) + others[0].astype(f32)) + (
            others[1].astype(f32) + others[2].astype(f32)
        )
    total = own.astype(f32)
    step = 1
    while step < count:
        sent = total.astype(bf16)
        total = sent.astype(f32) + swap(sent, "width", step).astype(f32)
        step *= 2
    return total


def plain_sum(value, axis):
    step = 1
    while step < lax.axis_size(axis):
        value = value + swap(value, axis, step)
        step *= 2
    return value


def mm(a, b, contract):
    return lax.dot_general(a, b, ((contract[:1], contract[1:]), ((), ())), preferred_element_type=f32)


def shards(activations, rest_recon, w_enc, b_enc, w_dec, b_dec):
    lat_count = lax.axis_size("lat")
    groups = lax.axis_size("groups")
    local_rows = activations.shape[0]
    row_scale = 1.0 / jnp.sqrt(f32(local_rows * lat_count))
    first = lax.axis_index("groups") == 0
    others = range(1, lat_count)

    xs = lat_gather(activations)
    centered = [(x.astype(f32) - b_dec).astype(bf16) for x in xs]
    codes = [
        jnp.maximum(width_sum(mm(c, w_enc, (1, 0))) + b_enc, 0.0).astype(bf16) for c in centered
    ]
    held = [codes[k] if k == 0 else swap(codes[k], "lat", k) for k in range(lat_count)]

    half = w_dec.shape[1] // groups
    mine = lax.dynamic_slice_in_dim(w_dec, lax.axis_index("groups") * half, half, axis=1)
    mine = after(mine, xs[2])
    mine = lat_gather(mine)
    other = [None] + [swap(mine[k], "groups", 1) for k in others]

    recon_mine = sum(mm(held[k], mine[k], (1, 0)) for k in others)
    recon_other = sum(mm(held[k], other[k], (1, 0)) for k in others)
    recon = mm(held[0], w_dec, (1, 0)) + jnp.concatenate(
        [
            jnp.where(first, recon_mine, recon_other),
            jnp.where(first, recon_other, recon_mine),
        ],
        axis=1,
    )
    error_rows = rest_recon.astype(f32) + recon + b_dec - activations.astype(f32)
    res_grad = (2.0 * row_scale * error_rows).astype(bf16)
    res_mine = jnp.where(first, res_grad[:, :half], res_grad[:, half:])
    res_other = jnp.where(first, res_grad[:, half:], res_grad[:, :half])

    parts = [mm(res_grad, w_dec, (1, 1))] + [
        mm(res_mine, mine[k], (1, 1)) + mm(res_other, other[k], (1, 1)) for k in others
    ]
    code_sums = [width_sum(p) for p in parts]
    code_sums = [code_sums[0]] + [
        swap(code_sums[k].astype(bf16), "lat", k).astype(f32) for k in others
    ]
    dec_float = w_dec.astype(f32)
    norms = jnp.sqrt(plain_sum(jnp.sum(dec_float * dec_float, axis=1), "width") + 1e-06)
    pre_grad = [
        jnp.where(c > 0, s + sparsity_coef * row_scale * norms, 0.0).astype(bf16)
        for c, s in zip(codes, code_sums)
    ]
    res = lat_gather(res_grad)

    grad_enc = sum(mm(c, p, (0, 0)) for c, p in zip(centered, pre_grad))
    grad_benc = sum(jnp.sum(p.astype(f32), axis=0) for p in pre_grad)
    code_total = sum(jnp.sum(c.astype(f32), axis=0) for c in codes)
    grad_dec = sum(mm(c, r, (0, 0)) for c, r in zip(codes, res))
    grad_dec = grad_dec + (sparsity_coef * row_scale * code_total / norms)[:, None] * dec_float
    enc_term = jnp.dot(w_enc.astype(f32), grad_benc, precision=lax.Precision.HIGHEST)
    grad_bdec = plain_sum(jnp.sum(res_grad.astype(f32), axis=0) - enc_term, "lat")
    return (grad_enc, grad_benc, grad_dec, grad_bdec)


def solution(mesh):
    placed = (
        P(("groups", "lat"), "width"),
        P(("groups", "lat"), "width"),
        P("width", "lat"),
        P("lat"),
        P("lat", "width"),
        P("width"),
    )
    return jax.shard_map(
        shards,
        mesh=mesh,
        in_specs=placed,
        out_specs=(
            P(("groups", "width"), "lat"),
            P(("groups", "lat")),
            P(("groups", "lat"), "width"),
            P(("groups", "width")),
        ),
        check_vma=False,
    )
```

```python
import jax
import jax.numpy as jnp
from jax import lax
from jax.experimental import pallas as pl
from jax.experimental.pallas import tpu as pltpu
from jax.sharding import PartitionSpec as P

sparsity_coef = 3.0
f32 = jnp.float32
bf16 = jnp.bfloat16


def swap(value, axis, distance):
    count = lax.axis_size(axis)
    return lax.ppermute(value, axis, [(i, i ^ distance) for i in range(count)])


def ring_pairs(steps):
    count = lax.axis_size("lat")
    order = [0] + list(range(1, count, 2)) + list(range(count - 2 + count % 2, 0, -2))
    return [(order[i], order[(i + steps) % count]) for i in range(count)]


def shift(value, steps):
    return lax.ppermute(value, "lat", ring_pairs(steps))


def shift_crossed(value, steps):
    width = lax.axis_size("width")
    pairs = [
        (a * width + w, b * width + (w ^ 1)) for a, b in ring_pairs(steps) for w in range(width)
    ]
    return lax.ppermute(value, ("lat", "width"), pairs)


def after(value, *earlier):
    return lax.optimization_barrier((value, *earlier))[0]


def stage(*values):
    return lax.optimization_barrier(values)


def width_sum(part):
    total = part.astype(f32)
    step = 1
    while step < lax.axis_size("width"):
        sent = lax.reduce_precision(total, 8, 7)
        total = sent + swap(sent.astype(bf16), "width", 2 * step - 1).astype(f32)
        step *= 2
    return total


def plain_sum(value, axis):
    step = 1
    while step < lax.axis_size(axis):
        value = value + swap(value, axis, step)
        step *= 2
    return value


def mm(a, b, contract):
    return lax.dot_general(a, b, ((contract[:1], contract[1:]), ((), ())), preferred_element_type=f32)


VMEM = pl.BlockSpec(memory_space=pltpu.VMEM)


def call(kernel, name, outs, *operands):
    return pl.pallas_call(
        kernel,
        out_shape=[jax.ShapeDtypeStruct(shape, kind) for shape, kind in outs],
        in_specs=[VMEM] * len(operands),
        out_specs=[VMEM] * len(outs),
        cost_estimate=pl.CostEstimate(flops=2 * 10**10, bytes_accessed=10**6, transcendentals=0),
        compiler_params=pltpu.CompilerParams(vmem_limit_bytes=40 * 2**20),
        name=name,
    )(*operands)


def part_of(x, b_dec, w_enc_t):
    def kernel(x_ref, b_ref, w_ref, centered_ref, part_ref):
        centered_ref[...] = (x_ref[...].astype(f32) - b_ref[...]).astype(bf16)
        part_ref[...] = mm(centered_ref[...], w_ref[...], (1, 1)).astype(bf16)

    rows, lat = x.shape[0], w_enc_t.shape[0]
    return call(kernel, "part_of", [(x.shape, bf16), ((rows, lat), bf16)], x, b_dec[None], w_enc_t)


def recon_start(x, rest, b_dec, held, w_dec):
    def kernel(x_ref, r_ref, b_ref, h_ref, w_ref, base):
        base[...] = (
            mm(h_ref[...], w_ref[...], (1, 0))
            + r_ref[...].astype(f32)
            + b_ref[...]
            - x_ref[...].astype(f32)
        )

    return call(kernel, "recon_start", [(x.shape, f32)], x, rest, b_dec[None], held, w_dec)[0]


def res_and_parts(scale, base, w_dec, held, mine, other):
    rows, cols = base.shape
    half, lat, count = cols // 2, w_dec.shape[0], len(held)

    def kernel(base_ref, w_ref, *refs):
        h, m, o = (refs[i * count : (i + 1) * count] for i in range(3))
        res_ref, part_ref = refs[3 * count :]
        first = lax.axis_index("groups") == 0
        r_mine = sum(mm(h[k][...], m[k][...], (1, 0)) for k in range(count))
        r_other = sum(mm(h[k][...], o[k][...], (1, 0)) for k in range(count))
        low = scale * (base_ref[:, :half] + jnp.where(first, r_mine, r_other))
        high = scale * (base_ref[:, half:] + jnp.where(first, r_other, r_mine))
        res_ref[:, :half] = low.astype(bf16)
        res_ref[:, half:] = high.astype(bf16)
        g_mine = jnp.where(first, low, high).astype(bf16)
        g_other = jnp.where(first, high, low).astype(bf16)
        part_ref[0] = mm(res_ref[...], w_ref[...], (1, 1)).astype(bf16)
        for k in range(count):
            part_ref[k + 1] = (
                mm(g_mine, m[k][...], (1, 1)) + mm(g_other, o[k][...], (1, 1))
            ).astype(bf16)

    outs = [((rows, cols), bf16), ((count + 1, rows, lat), bf16)]
    return call(kernel, "res_and_parts", outs, base, w_dec, *held, *mine, *other)


def dec_add(total, codes, res):
    count = len(codes)

    def kernel(*refs):
        c, r = refs[:count], refs[count : 2 * count]
        value = sum(mm(c[k][...], r[k][...], (0, 0)) for k in range(count))
        if total is not None:
            value = refs[2 * count][...] + value
        refs[-1][...] = value

    outs = [((codes[0].shape[1], res[0].shape[1]), f32)]
    start = [] if total is None else [total]
    return call(kernel, "dec_add", outs, *codes, *res, *start)[0]


def pre_grads(codes, back, threshold, w_enc_t, res):
    count = len(codes)

    def kernel(n_ref, w_ref, res_ref, *refs):
        masks, sums, grads = (refs[i * count : (i + 1) * count] for i in range(3))
        bias, share = refs[3 * count :]
        total = 0.0
        for m, s, out in zip(masks, sums, grads):
            g = jnp.where(m[...].astype(f32) > 0, s[...].astype(f32) + n_ref[...], 0.0)
            out[...] = g.astype(bf16)
            total = total + jnp.sum(out[...].astype(f32), axis=0, keepdims=True)
        bias[...] = total
        share[...] = jnp.sum(res_ref[...].astype(f32), axis=0, keepdims=True) - lax.dot_general(
            total,
            w_ref[...].astype(f32),
            (((1,), (0,)), ((), ())),
            precision=lax.Precision.HIGHEST,
            preferred_element_type=f32,
        )

    lat, cols = w_enc_t.shape
    outs = [(codes[0].shape, bf16)] * count + [((1, lat), f32), ((1, cols), f32)]
    *grads, bias, share = call(
        kernel, "pre_grads", outs, threshold[None], w_enc_t, res, *codes, *back
    )
    return grads, bias[0], share[0]


def enc_end(centered, grads):
    count = len(grads)

    def kernel(*refs):
        g, c = refs[:count], refs[count : 2 * count]
        refs[-1][...] = sum(mm(g[k][...], c[k][...], (0, 0)) for k in range(count))

    outs = [((grads[0].shape[1], centered[0].shape[1]), f32)]
    return call(kernel, "enc_end", outs, *grads, *centered)[0]


def square_sums(w_dec):
    dec_float = w_dec.astype(f32)
    return plain_sum(jnp.sum(dec_float * dec_float, axis=1), "width")


def shards(activations, rest_recon, w_enc, b_enc, w_dec, b_dec):
    count = lax.axis_size("lat")
    row_scale = float((activations.shape[0] * count) ** -0.5)
    w_enc_t = w_enc.T
    half = w_dec.shape[1] // 2
    mine_own = lax.dynamic_slice_in_dim(w_dec, lax.axis_index("groups") * half, half, axis=1)

    def to_codes(total):
        return jnp.maximum(total + b_enc, 0.0).astype(bf16)

    xs, mine = [activations], [mine_own]
    for j in range(1, count):
        xs.append(shift(xs[-1], 1))
    squares = square_sums(after(w_dec, xs[1]))
    mine.append(shift(after(mine_own, xs[1]), -1))
    xs[-1], mine[1], squares = stage(xs[-1], mine[1], squares)
    for j in range(2, count):
        mine.append(shift(mine[-1], -1))
    other = [swap(m, "groups", 1) for m in mine[1:]]

    centered, codes = [], []
    for x in xs:
        c, part = part_of(x, b_dec, w_enc_t)
        centered.append(c)
        codes.append(to_codes(width_sum(part)))
    held = codes[:1] + [shift_crossed(codes[j], -j) for j in range(1, count)]

    base = recon_start(activations, rest_recon, b_dec, held[0], w_dec)
    res_grad, sums = res_and_parts(2.0 * row_scale, base, w_dec, held[1:], mine[1:], other)

    res = [res_grad]
    for j in range(1, count):
        res.append(shift(res[-1], 1))
    sums = width_sum(sums).astype(bf16)
    back = [sums[0]] + [shift_crossed(sums[j], j) for j in range(1, count)]
    norms = jnp.sqrt(squares + 1e-06)
    grads, grad_benc, share = pre_grads(
        codes, back, sparsity_coef * row_scale * norms, w_enc_t, res_grad
    )
    grad_bdec = plain_sum(share, "lat")
    grad_enc = enc_end(centered, grads).T
    code_total = sum(jnp.sum(c.astype(f32), axis=0) for c in codes)
    sparsity = (sparsity_coef * row_scale * code_total / norms)[:, None] * w_dec.astype(f32)
    grad_dec = dec_add(sparsity, codes[:2], res[:2])
    for j in range(2, count):
        grad_dec = dec_add(grad_dec, codes[j : j + 1], res[j : j + 1])
    return (grad_enc, grad_benc, grad_dec, grad_bdec)


def solution(mesh):
    placed = (
        P(("groups", "lat"), "width"),
        P(("groups", "lat"), "width"),
        P("width", "lat"),
        P("lat"),
        P("lat", "width"),
        P("width"),
    )
    return jax.shard_map(
        shards,
        mesh=mesh,
        in_specs=placed,
        out_specs=(
            P(("groups", "width"), "lat"),
            P(("groups", "lat")),
            P(("groups", "lat"), "width"),
            P(("groups", "width")),
        ),
        check_vma=False,
    )
```

```python
import jax
import jax.numpy as jnp
from jax import lax
from jax.experimental import pallas as pl
from jax.experimental.pallas import tpu as pltpu
from jax.sharding import PartitionSpec as P

sparsity_coef = 3.0
f32 = jnp.float32
bf16 = jnp.bfloat16


def swap(value, axis, distance):
    count = lax.axis_size(axis)
    return lax.ppermute(value, axis, [(i, i ^ distance) for i in range(count)])


def swap_crossed(value, distance):
    lat, width = lax.axis_size("lat"), lax.axis_size("width")
    pairs = [
        (z * width + w, (z ^ distance) * width + (w ^ 1)) for z in range(lat) for w in range(width)
    ]
    return lax.ppermute(value, ("lat", "width"), pairs)


def after(value, *earlier):
    return lax.optimization_barrier((value, *earlier))[0]


def stage(*values):
    return lax.optimization_barrier(values)


def keeps_low():
    index, odd = lax.axis_index("width"), 0
    for bit in range((lax.axis_size("width") - 1).bit_length()):
        odd = odd ^ ((index >> bit) & 1)
    return odd == 0


def pair_sum(keep, send):
    return keep.astype(f32) + swap(send, "width", 1).astype(f32)


def rest_sum(total):
    step = 3
    while step < lax.axis_size("width") * 3 // 2:
        sent = lax.reduce_precision(total, 8, 7)
        total = sent + swap(sent.astype(bf16), "width", step).astype(f32)
        step *= 2
    return total


def join(kept, other):
    low = keeps_low()
    first, second = jnp.where(low, kept, other), jnp.where(low, other, kept)
    return jnp.concatenate([first, second], axis=0)


def plain_sum(value, axis):
    step = 1
    while step < lax.axis_size(axis):
        value = value + swap(value, axis, step)
        step *= 2
    return value


def mm(a, b, contract):
    return lax.dot_general(a, b, ((contract[:1], contract[1:]), ((), ())), preferred_element_type=f32)


VMEM = pl.BlockSpec(memory_space=pltpu.VMEM)


def call(kernel, name, outs, *operands):
    return pl.pallas_call(
        kernel,
        out_shape=[jax.ShapeDtypeStruct(shape, kind) for shape, kind in outs],
        in_specs=[VMEM] * len(operands),
        out_specs=[VMEM] * len(outs),
        cost_estimate=pl.CostEstimate(flops=10**6, bytes_accessed=10**6, transcendentals=0),
        compiler_params=pltpu.CompilerParams(vmem_limit_bytes=24 * 2**20),
        name=name,
    )(*operands)


def split(part, keep_ref, send_ref):
    rows = part.shape[0] // 2
    low = keeps_low()
    keep_ref[...] = jnp.where(low, part[:rows], part[rows:]).astype(bf16)
    send_ref[...] = jnp.where(low, part[rows:], part[:rows]).astype(bf16)


def part_of(x, b_dec, w_enc_t):
    rows, lat = x.shape[0] // 2, w_enc_t.shape[0]

    def kernel(x_ref, b_ref, w_ref, centered_ref, keep_ref, send_ref):
        centered_ref[...] = (x_ref[...].astype(f32) - b_ref[...]).astype(bf16)
        split(mm(centered_ref[...], w_ref[...], (1, 1)), keep_ref, send_ref)

    outs = [(x.shape, bf16), ((rows, lat), bf16), ((rows, lat), bf16)]
    return call(kernel, "part_of", outs, x, b_dec[None], w_enc_t)


def error_start(x, rest, b_dec):
    def kernel(x_ref, r_ref, b_ref, base):
        base[...] = r_ref[...].astype(f32) + b_ref[...] - x_ref[...].astype(f32)

    return call(kernel, "error_start", [(x.shape, f32)], x, rest, b_dec[None])[0]


def res_and_parts(scale, base, w_dec, codes, codes_other, crossed, crossed_other, mine, other):
    rows, cols = base.shape
    half, lat, count = cols // 2, w_dec.shape[0], len(mine)

    def kernel(base_ref, w_ref, c_ref, c_other_ref, x_ref, x_other_ref, *refs):
        m, o = refs[:count], refs[count : 2 * count]
        codes_ref, res_ref, keep_ref, send_ref = refs[2 * count :]
        first = lax.axis_index("groups") == 0
        for k in range(count + 1):
            codes_ref[k] = join(c_ref[k].astype(f32), c_other_ref[k].astype(f32)).astype(bf16)
        start = base_ref[...] + mm(codes_ref[0], w_ref[...], (1, 0))
        held = [
            join(x_other_ref[k].astype(f32), x_ref[k].astype(f32)).astype(bf16)
            for k in range(count)
        ]
        r_mine = sum(mm(held[k], m[k][...], (1, 0)) for k in range(count))
        r_other = sum(mm(held[k], o[k][...], (1, 0)) for k in range(count))
        low = scale * (start[:, :half] + jnp.where(first, r_mine, r_other))
        high = scale * (start[:, half:] + jnp.where(first, r_other, r_mine))
        res_ref[:, :half] = low.astype(bf16)
        res_ref[:, half:] = high.astype(bf16)
        g_mine = jnp.where(first, low, high).astype(bf16)
        g_other = jnp.where(first, high, low).astype(bf16)
        split(mm(res_ref[...], w_ref[...], (1, 1)), keep_ref.at[0], send_ref.at[0])
        for k in range(count):
            part = mm(g_mine, m[k][...], (1, 1)) + mm(g_other, o[k][...], (1, 1))
            split(part, keep_ref.at[k + 1], send_ref.at[k + 1])

    parts = ((count + 1, rows // 2, lat), bf16)
    outs = [((count + 1, rows, lat), bf16), ((rows, cols), bf16), parts, parts]
    return call(
        kernel, "res_and_parts", outs,
        base, w_dec, codes, codes_other, crossed, crossed_other, *mine, *other,
    )


def dec_add(total, codes, res, *shares):
    count = len(res)

    def kernel(total_ref, c_ref, *refs):
        value = sum(mm(c_ref[k], refs[k][...], (0, 0)) for k in range(count))
        refs[count + len(shares)][...] = total_ref[...] + value
        if shares:
            refs[-1][...] = refs[count][...] + refs[count + 1][...]

    outs = [(total.shape, f32)] + [(s.shape, f32) for s in shares[:1]]
    return call(kernel, "dec_add", outs, total, codes, *res, *shares)


def pre_grads(codes, sums, sums_other, crossed, crossed_other, threshold, w_enc_t, res):
    count = codes.shape[0]

    def kernel(n_ref, w_ref, res_ref, c_ref, s_ref, so_ref, x_ref, xo_ref, out, bias, share):
        total = 0.0
        for k in range(count):
            if k:
                back = join(xo_ref[k - 1].astype(f32), x_ref[k - 1].astype(f32))
            else:
                back = join(s_ref[0].astype(f32), so_ref[0].astype(f32))
            g = jnp.where(c_ref[k].astype(f32) > 0, back + n_ref[...], 0.0)
            out[k] = g.astype(bf16)
            total = total + jnp.sum(out[k].astype(f32), axis=0, keepdims=True)
        bias[...] = total
        high = total.astype(bf16)
        rest = total - high.astype(f32)
        mid = rest.astype(bf16)
        low = (rest - mid.astype(f32)).astype(bf16)
        row = lax.broadcasted_iota(jnp.int32, (8, total.shape[1]), 0)
        pieces = jnp.where(row == 0, high.astype(f32), jnp.where(row == 1, mid.astype(f32), 0.0))
        pieces = jnp.where(row == 2, low.astype(f32), pieces).astype(bf16)
        product = jnp.sum(mm(pieces, w_ref[...], (1, 0)), axis=0, keepdims=True)
        share[...] = jnp.sum(res_ref[...].astype(f32), axis=0, keepdims=True) - product

    lat, cols = w_enc_t.shape
    outs = [(codes.shape, bf16), ((1, lat), f32), ((1, cols), f32)]
    grads, bias, share = call(
        kernel, "pre_grads", outs,
        threshold[None], w_enc_t, res, codes, sums, sums_other, crossed, crossed_other,
    )
    return grads, bias[0], share


def enc_end(centered, grads):
    count = len(centered)

    def kernel(g_ref, *refs):
        refs[-1][...] = sum(mm(g_ref[k], refs[k][...], (0, 0)) for k in range(count))

    outs = [((grads.shape[2], centered[0].shape[1]), f32)]
    return call(kernel, "enc_end", outs, grads, *centered)[0]


def halves(stacked, first):
    return stacked[:first], stacked[first:]


def shards(activations, rest_recon, w_enc, b_enc, w_dec, b_dec):
    count = lax.axis_size("lat")
    rows = activations.shape[0]
    row_scale = float((rows * count) ** -0.5)
    w_enc_t = w_enc.T
    half = w_dec.shape[1] // 2
    late = 2
    order = [k for k in range(count) if k != late] + [late]
    early = order[1:-1]

    def early_swaps(block):
        return [swap(block, "lat", k) for k in early]

    def late_swap(block, swapped):
        return swap(swapped[-1], "lat", 1) if count == 4 else swap(block, "lat", late)

    mine_own = lax.dynamic_slice_in_dim(w_dec, lax.axis_index("groups") * half, half, axis=1)
    xs, mine = early_swaps(activations), early_swaps(mine_own)
    arrived = stage(*xs, *mine)
    xs, mine = list(arrived[: len(xs)]), list(arrived[len(xs) :])

    final, mine_late = late_swap(activations, xs), late_swap(mine_own, mine)
    other = [swap(m, "groups", 1) for m in mine]
    dec_float = after(w_dec, mine[0]).astype(f32)
    squares = jnp.sum(dec_float * dec_float, axis=1)
    squares = squares + swap(squares, "width", 1)
    base = error_start(activations, rest_recon, b_dec)
    centered, keep, send = zip(*(part_of(x, b_dec, w_enc_t) for x in [activations, *xs]))
    total = pair_sum(jnp.stack(keep), jnp.stack(send))
    final, mine_late, squares, base, total, *other = stage(
        final, mine_late, squares, base, total, *other
    )
    mine.append(mine_late)

    last_centered, last_keep, last_send = part_of(final, b_dec, w_enc_t)
    centered += (last_centered,)
    total = jnp.concatenate([total, pair_sum(last_keep, last_send)[None]])
    codes = jnp.maximum(rest_sum(total) + b_enc, 0.0).astype(bf16)
    other.append(swap(mine_late, "groups", 1))
    codes, other[-1] = stage(codes, other[-1])
    crossed = jnp.stack([swap_crossed(codes[i], k) for i, k in enumerate(order) if k])
    codes_other = swap(codes, "width", 1)
    step = 3
    while step < lax.axis_size("width") * 3 // 2:
        squares = squares + swap(after(squares, codes), "width", step)
        step *= 2
    crossed, codes_other, squares = stage(crossed, codes_other, squares)
    crossed_other = swap(crossed, "width", 1)
    codes, res_grad, keep, send = res_and_parts(
        2.0 * row_scale, base, w_dec, codes, codes_other, crossed, crossed_other, mine, other
    )

    res = early_swaps(res_grad)
    sums = rest_sum(pair_sum(keep, send)).astype(bf16)
    crossed = jnp.stack([swap_crossed(sums[i], k) for i, k in enumerate(order) if k])
    sums_other = swap(sums[:1], "width", 1)
    res[-1], crossed, sums_other = stage(res[-1], crossed, sums_other)
    norms = jnp.sqrt(squares + 1e-06)
    grads, grad_benc, share = pre_grads(
        codes,
        sums[:1],
        sums_other,
        crossed,
        swap(crossed, "width", 1),
        sparsity_coef * row_scale * norms,
        w_enc_t,
        res_grad,
    )
    step = 1
    while 2 * step < count:
        share = share + swap(share, "lat", step)
        step *= 2
    share, *res = stage(share, *res)
    res_late = late_swap(res_grad, res)
    grad_enc = enc_end(centered, grads).T
    code_total = jnp.sum(codes.astype(f32), axis=(0, 1))
    sparsity = (sparsity_coef * row_scale * code_total / norms)[:, None] * w_dec.astype(f32)
    (grad_dec,) = dec_add(sparsity, codes[:-1], [res_grad, *res])
    grad_dec, grad_bdec = dec_add(
        grad_dec, codes[-1:], [res_late], share, swap(share, "lat", step)
    )
    return (grad_enc, grad_benc, grad_dec, grad_bdec[0])


def solution(mesh):
    placed = (
        P(("groups", "lat"), "width"),
        P(("groups", "lat"), "width"),
        P("width", "lat"),
        P("lat"),
        P("lat", "width"),
        P("width"),
    )
    return jax.shard_map(
        shards,
        mesh=mesh,
        in_specs=placed,
        out_specs=(
            P(("groups", "width"), "lat"),
            P(("groups", "lat")),
            P(("groups", "lat"), "width"),
            P(("groups", "width")),
        ),
        check_vma=False,
    )
```

```python
import jax
import jax.numpy as jnp
from jax import lax
from jax.experimental import pallas as pl
from jax.experimental.pallas import tpu as pltpu
from jax.sharding import PartitionSpec as P

sparsity_coef = 3.0
f32 = jnp.float32
bf16 = jnp.bfloat16


def swap(value, axis, distance):
    count = lax.axis_size(axis)
    return lax.ppermute(value, axis, [(i, i ^ distance) for i in range(count)])


def after(value, *earlier):
    return lax.optimization_barrier((value, *earlier))[0]


def stage(*values):
    return lax.optimization_barrier(values)


def width_sum(part):
    total, step = part.astype(f32), 1
    while step < lax.axis_size("width"):
        sent = lax.reduce_precision(total, 8, 7)
        total = sent + swap(sent.astype(bf16), "width", 2 * step - 1).astype(f32)
        step *= 2
    return total


def plain_sum(value, axis):
    step = 1
    while step < lax.axis_size(axis):
        value = value + swap(value, axis, step)
        step *= 2
    return value


def mm(a, b, contract):
    return lax.dot_general(a, b, ((contract[:1], contract[1:]), ((), ())), preferred_element_type=f32)


VMEM = pl.BlockSpec(memory_space=pltpu.VMEM)


def call(kernel, name, outs, *operands):
    return pl.pallas_call(
        kernel,
        out_shape=[jax.ShapeDtypeStruct(shape, kind) for shape, kind in outs],
        in_specs=[VMEM] * len(operands),
        out_specs=[VMEM] * len(outs),
        cost_estimate=pl.CostEstimate(flops=10**6, bytes_accessed=10**6, transcendentals=0),
        compiler_params=pltpu.CompilerParams(vmem_limit_bytes=24 * 2**20),
        name=name,
    )(*operands)


def part_of(x, b_dec, w_enc_t):
    def kernel(x_ref, b_ref, w_ref, centered_ref, part_ref):
        centered_ref[...] = (x_ref[...].astype(f32) - b_ref[...]).astype(bf16)
        part_ref[...] = mm(centered_ref[...], w_ref[...], (1, 1)).astype(bf16)

    outs = [(x.shape, bf16), ((x.shape[0], w_enc_t.shape[0]), bf16)]
    return call(kernel, "part_of", outs, x, b_dec[None], w_enc_t)


def recon_of(codes, w_dec, *sums):
    def kernel(c_ref, w_ref, *refs):
        value = mm(c_ref[...], w_ref[...], (1, 0))
        for ref in refs[:-1]:
            value = value + ref[...].astype(f32)
        refs[-1][...] = value.astype(bf16)

    outs = [((codes.shape[0], w_dec.shape[1]), bf16)]
    return call(kernel, "recon_of", outs, codes, w_dec, *sums)[0]


def res_of(scale, x, rest, b_dec, codes, w_dec, sums):
    def kernel(x_ref, r_ref, b_ref, c_ref, w_ref, *refs):
        value = r_ref[...].astype(f32) + b_ref[...] - x_ref[...].astype(f32)
        value = value + mm(c_ref[...], w_ref[...], (1, 0))
        for ref in refs[:-2]:
            value = value + ref[...].astype(f32)
        res_ref, part_ref = refs[-2:]
        res_ref[...] = (scale * value).astype(bf16)
        part_ref[...] = mm(res_ref[...], w_ref[...], (1, 1)).astype(bf16)

    outs = [(x.shape, bf16), (codes.shape, bf16)]
    return call(kernel, "res_of", outs, x, rest, b_dec[None], codes, w_dec, *sums)


def code_part(res, w_dec):
    def kernel(r_ref, w_ref, out):
        out[...] = mm(r_ref[...], w_ref[...], (1, 1)).astype(bf16)

    return call(kernel, "code_part", [((res.shape[0], w_dec.shape[0]), bf16)], res, w_dec)[0]


def dec_add(total, codes, res, *shares):
    count = len(res)

    def kernel(total_ref, *refs):
        value = sum(mm(refs[k][...], refs[count + k][...], (0, 0)) for k in range(count))
        refs[2 * count + len(shares)][...] = total_ref[...] + value
        if shares:
            refs[-1][...] = refs[2 * count][...] + refs[2 * count + 1][...]

    outs = [(total.shape, f32)] + [(s.shape, f32) for s in shares[:1]]
    return call(kernel, "dec_add", outs, total, *codes, *res, *shares)


def pre_grads(codes, sums, threshold, w_enc_t, res):
    count = len(codes)

    def kernel(n_ref, w_ref, res_ref, *refs):
        c, s = refs[:count], refs[count : 2 * count]
        out, bias, share = refs[2 * count :]
        total = 0.0
        for k in range(count):
            g = jnp.where(c[k][...].astype(f32) > 0, s[k][...] + n_ref[...], 0.0)
            out[k] = g.astype(bf16)
            total = total + jnp.sum(out[k].astype(f32), axis=0, keepdims=True)
        bias[...] = total
        high = total.astype(bf16)
        rest = total - high.astype(f32)
        mid = rest.astype(bf16)
        low = (rest - mid.astype(f32)).astype(bf16)
        row = lax.broadcasted_iota(jnp.int32, (8, total.shape[1]), 0)
        pieces = jnp.where(row == 0, high.astype(f32), jnp.where(row == 1, mid.astype(f32), 0.0))
        pieces = jnp.where(row == 2, low.astype(f32), pieces).astype(bf16)
        product = jnp.sum(mm(pieces, w_ref[...], (1, 0)), axis=0, keepdims=True)
        share[...] = jnp.sum(res_ref[...].astype(f32), axis=0, keepdims=True) - product

    lat, cols = w_enc_t.shape
    outs = [((count, *codes[0].shape), bf16), ((1, lat), f32), ((1, cols), f32)]
    grads, bias, share = call(
        kernel, "pre_grads", outs, threshold[None], w_enc_t, res, *codes, *sums
    )
    return grads, bias[0], share


def enc_end(centered, grads):
    count = len(centered)

    def kernel(g_ref, *refs):
        refs[-1][...] = sum(mm(g_ref[k], refs[k][...], (0, 0)) for k in range(count))

    outs = [((grads.shape[2], centered[0].shape[1]), f32)]
    return call(kernel, "enc_end", outs, grads, *centered)[0]


def square_sums(w_dec):
    dec_float = w_dec.astype(f32)
    value, step = jnp.sum(dec_float * dec_float, axis=1), 1
    while step < lax.axis_size("width"):
        value = value + swap(value, "width", 2 * step - 1)
        step *= 2
    return value


def shards(activations, rest_recon, w_enc, b_enc, w_dec, b_dec):
    count = lax.axis_size("lat")
    line = count == 4
    others = range(1, count)
    row_scale = float((activations.shape[0] * count) ** -0.5)
    w_enc_t = w_enc.T

    def lat_swap(block, distance):
        return swap(block, "lat", distance)

    xs = [activations] + [lat_swap(activations, k) if k != 2 or not line else None for k in others]
    centered, parts, codes = [None] * count, [None] * count, [None] * count

    def add_parts(blocks):
        for k in blocks:
            centered[k], parts[k] = part_of(xs[k], b_dec, w_enc_t)

    def add_codes(blocks, total):
        for i, k in enumerate(blocks):
            codes[k] = jnp.maximum(total[i] + b_enc, 0.0).astype(bf16)

    def sum_parts(blocks):
        return width_sum(jnp.stack([parts[k] for k in blocks]))

    add_parts([0])
    if line:
        xs[1], xs[3], centered[0], parts[0] = stage(xs[1], xs[3], centered[0], parts[0])
        xs[2] = lat_swap(xs[3], 1)
        add_parts([1, 3])
        xs[2], total = stage(xs[2], sum_parts([3]))
        add_codes([3], total)
        passed = lat_swap(recon_of(codes[3], w_dec), 1)
        add_parts([2])
        passed, total = stage(passed, sum_parts([0, 1, 2]))
        add_codes([0, 1, 2], total)
        sums = [
            lat_swap(recon_of(codes[1], w_dec), 1),
            lat_swap(recon_of(codes[2], w_dec, passed), 2),
        ]
    else:
        add_parts(others)
        add_codes(range(count), sum_parts(range(count)))
        sums = [lat_swap(recon_of(codes[k], w_dec), k) for k in others]
    res_grad, part = res_of(
        2.0 * row_scale, activations, rest_recon, b_dec, codes[0], w_dec, sums
    )

    res = [res_grad] + [lat_swap(res_grad, k) if k != 3 or not line else None for k in others]
    if line:
        res[1], res[2] = stage(res[1], res[2])
        res[3] = lat_swap(res[2], 1)
    parts = [part] + [code_part(res[k], w_dec) for k in others]
    early = width_sum(jnp.stack(parts[:-1]))
    code_sums = [early[k] for k in range(count - 1)] + [width_sum(parts[-1])]
    squares = square_sums(after(w_dec, xs[1]))
    norms = jnp.sqrt(squares + 1e-06)
    grads, grad_benc, share = pre_grads(
        codes, code_sums, sparsity_coef * row_scale * norms, w_enc_t, res_grad
    )
    step = 1
    while 2 * step < count:
        share = share + lat_swap(share, step)
        step *= 2
    grad_enc = enc_end(centered, grads).T
    code_total = sum(jnp.sum(c.astype(f32), axis=0) for c in codes)
    sparsity = (sparsity_coef * row_scale * code_total / norms)[:, None] * w_dec.astype(f32)
    (grad_dec,) = dec_add(sparsity, codes, res)
    grad_bdec = share + lat_swap(share, step)
    return (grad_enc, grad_benc, grad_dec, grad_bdec[0])


def solution(mesh):
    placed = (
        P(("groups", "lat"), "width"),
        P(("groups", "lat"), "width"),
        P("width", "lat"),
        P("lat"),
        P("lat", "width"),
        P("width"),
    )
    return jax.shard_map(
        shards,
        mesh=mesh,
        in_specs=placed,
        out_specs=(
            P(("groups", "width"), "lat"),
            P(("groups", "lat")),
            P(("groups", "lat"), "width"),
            P(("groups", "width")),
        ),
        check_vma=False,
    )
```

```python
import jax
import jax.numpy as jnp
from jax import lax
from jax.experimental import pallas as pl
from jax.experimental.pallas import tpu as pltpu
from jax.sharding import PartitionSpec as P

sparsity_coef = 3.0
f32 = jnp.float32
bf16 = jnp.bfloat16


def swap(value, axis, distance):
    count = lax.axis_size(axis)
    return lax.ppermute(value, axis, [(i, i ^ distance) for i in range(count)])


def after(value, *earlier):
    return lax.optimization_barrier((value, *earlier))[0]


def stage(*values):
    return lax.optimization_barrier(values)


def width_sum(part):
    total, step = part.astype(f32), 1
    while step < lax.axis_size("width"):
        sent = lax.reduce_precision(total, 8, 7)
        total = sent + swap(sent.astype(bf16), "width", 2 * step - 1).astype(f32)
        step *= 2
    return total


def plain_sum(value, axis):
    step = 1
    while step < lax.axis_size(axis):
        value = value + swap(value, axis, step)
        step *= 2
    return value


def keeps_low():
    index, odd = lax.axis_index("width"), 0
    for bit in range((lax.axis_size("width") - 1).bit_length()):
        odd = odd ^ ((index >> bit) & 1)
    return odd == 0


def half_sum(part):
    rows, low = part.shape[0] // 2, keeps_low()
    keep = jnp.where(low, part[:rows], part[rows:])
    send = jnp.where(low, part[rows:], part[:rows])
    total, step = keep.astype(f32) + swap(send, "width", 1).astype(f32), 3
    while step < lax.axis_size("width") * 3 // 2:
        sent = lax.reduce_precision(total, 8, 7)
        total = sent + swap(sent.astype(bf16), "width", step).astype(f32)
        step *= 2
    return total


def join(kept):
    low, other = keeps_low(), swap(kept, "width", 1)
    return jnp.concatenate([jnp.where(low, kept, other), jnp.where(low, other, kept)])


def mm(a, b, contract):
    return lax.dot_general(a, b, ((contract[:1], contract[1:]), ((), ())), preferred_element_type=f32)


VMEM = pl.BlockSpec(memory_space=pltpu.VMEM)


def call(kernel, name, outs, *operands):
    return pl.pallas_call(
        kernel,
        out_shape=[jax.ShapeDtypeStruct(shape, kind) for shape, kind in outs],
        in_specs=[VMEM] * len(operands),
        out_specs=[VMEM] * len(outs),
        cost_estimate=pl.CostEstimate(flops=10**6, bytes_accessed=10**6, transcendentals=0),
        compiler_params=pltpu.CompilerParams(vmem_limit_bytes=24 * 2**20),
        name=name,
    )(*operands)


def part_of(x, b_dec, w_enc_t):
    def kernel(x_ref, b_ref, w_ref, centered_ref, part_ref):
        centered_ref[...] = (x_ref[...].astype(f32) - b_ref[...]).astype(bf16)
        part_ref[...] = mm(centered_ref[...], w_ref[...], (1, 1)).astype(bf16)

    outs = [(x.shape, bf16), ((x.shape[0], w_enc_t.shape[0]), bf16)]
    return call(kernel, "part_of", outs, x, b_dec[None], w_enc_t)


def recon_of(codes, w_dec, *sums):
    def kernel(c_ref, w_ref, *refs):
        value = mm(c_ref[...], w_ref[...], (1, 0))
        for ref in refs[:-1]:
            value = value + ref[...].astype(f32)
        refs[-1][...] = value.astype(bf16)

    outs = [((codes.shape[0], w_dec.shape[1]), bf16)]
    return call(kernel, "recon_of", outs, codes, w_dec, *sums)[0]


def res_of(scale, x, rest, b_dec, codes, w_dec, sums):
    def kernel(x_ref, r_ref, b_ref, c_ref, w_ref, *refs):
        value = r_ref[...].astype(f32) + b_ref[...] - x_ref[...].astype(f32)
        value = value + mm(c_ref[...], w_ref[...], (1, 0))
        for ref in refs[:-2]:
            value = value + ref[...].astype(f32)
        res_ref, part_ref = refs[-2:]
        res_ref[...] = (scale * value).astype(bf16)
        part_ref[...] = mm(res_ref[...], w_ref[...], (1, 1)).astype(bf16)

    outs = [(x.shape, bf16), (codes.shape, bf16)]
    return call(kernel, "res_of", outs, x, rest, b_dec[None], codes, w_dec, *sums)


def code_part(res, w_dec):
    def kernel(r_ref, w_ref, out):
        out[...] = mm(r_ref[...], w_ref[...], (1, 1)).astype(bf16)

    return call(kernel, "code_part", [((res.shape[0], w_dec.shape[0]), bf16)], res, w_dec)[0]


def dec_add(total, codes, res, *shares):
    count = len(res)

    def kernel(total_ref, *refs):
        value = sum(mm(refs[k][...], refs[count + k][...], (0, 0)) for k in range(count))
        refs[2 * count + len(shares)][...] = total_ref[...] + value
        if shares:
            refs[-1][...] = refs[2 * count][...] + refs[2 * count + 1][...]

    outs = [(total.shape, f32)] + [(s.shape, f32) for s in shares[:1]]
    return call(kernel, "dec_add", outs, total, *codes, *res, *shares)


def pre_grads(codes, sums, threshold, w_enc_t, res):
    count = len(codes)

    def kernel(n_ref, w_ref, res_ref, *refs):
        c, s = refs[:count], refs[count : 2 * count]
        out, bias, share = refs[2 * count :]
        total = 0.0
        for k in range(count):
            g = jnp.where(c[k][...].astype(f32) > 0, s[k][...] + n_ref[...], 0.0)
            out[k] = g.astype(bf16)
            total = total + jnp.sum(out[k].astype(f32), axis=0, keepdims=True)
        bias[...] = total
        high = total.astype(bf16)
        rest = total - high.astype(f32)
        mid = rest.astype(bf16)
        low = (rest - mid.astype(f32)).astype(bf16)
        row = lax.broadcasted_iota(jnp.int32, (8, total.shape[1]), 0)
        pieces = jnp.where(row == 0, high.astype(f32), jnp.where(row == 1, mid.astype(f32), 0.0))
        pieces = jnp.where(row == 2, low.astype(f32), pieces).astype(bf16)
        product = jnp.sum(mm(pieces, w_ref[...], (1, 0)), axis=0, keepdims=True)
        share[...] = jnp.sum(res_ref[...].astype(f32), axis=0, keepdims=True) - product

    lat, cols = w_enc_t.shape
    outs = [((count, *codes[0].shape), bf16), ((1, lat), f32), ((1, cols), f32)]
    grads, bias, share = call(
        kernel, "pre_grads", outs, threshold[None], w_enc_t, res, *codes, *sums
    )
    return grads, bias[0], share


def enc_end(centered, grads):
    count = len(centered)

    def kernel(g_ref, *refs):
        refs[-1][...] = sum(mm(g_ref[k], refs[k][...], (0, 0)) for k in range(count))

    outs = [((grads.shape[2], centered[0].shape[1]), f32)]
    return call(kernel, "enc_end", outs, grads, *centered)[0]


def square_sums(w_dec):
    dec_float = w_dec.astype(f32)
    value, step = jnp.sum(dec_float * dec_float, axis=1), 1
    while step < lax.axis_size("width"):
        value = value + swap(value, "width", 2 * step - 1)
        step *= 2
    return value


def shards(activations, rest_recon, w_enc, b_enc, w_dec, b_dec):
    count = lax.axis_size("lat")
    line = count == 4
    others = range(1, count)
    row_scale = float((activations.shape[0] * count) ** -0.5)
    w_enc_t = w_enc.T

    def lat_swap(block, distance):
        return swap(block, "lat", distance)

    xs = [activations] + [lat_swap(activations, k) if k != 2 or not line else None for k in others]
    centered, parts, codes = [None] * count, [None] * count, [None] * count

    def add_parts(blocks):
        for k in blocks:
            centered[k], parts[k] = part_of(xs[k], b_dec, w_enc_t)

    def add_codes(blocks, total):
        for i, k in enumerate(blocks):
            codes[k] = jnp.maximum(total[i] + b_enc, 0.0).astype(bf16)

    def sum_parts(blocks):
        return width_sum(jnp.stack([parts[k] for k in blocks]))

    add_parts([0])
    if line:
        xs[3], xs[1], centered[0], parts[0] = stage(xs[3], xs[1], centered[0], parts[0])
        xs[2] = lat_swap(xs[3], 1)
        add_parts([1, 3])
        kept = jnp.maximum(half_sum(parts[3]) + b_enc, 0.0).astype(bf16)
        xs[2], kept = stage(xs[2], kept)
        codes[3] = join(kept)
        passed = lat_swap(recon_of(codes[3], w_dec), 1)
        add_parts([2])
        passed, total = stage(passed, sum_parts([0, 1, 2]))
        add_codes([0, 1, 2], total)
        onward = recon_of(codes[2], w_dec, passed)
        sums = [lat_swap(recon_of(after(codes[1], onward), w_dec), 1), lat_swap(onward, 2)]
    else:
        add_parts(others)
        add_codes(range(count), sum_parts(range(count)))
        sums = [lat_swap(recon_of(codes[k], w_dec), k) for k in others]
    res_grad, part = res_of(
        2.0 * row_scale, activations, rest_recon, b_dec, codes[0], w_dec, sums
    )

    res = [res_grad] + [lat_swap(res_grad, k) if k != 3 or not line else None for k in others]
    if line:
        res[2], res[1] = stage(res[2], res[1])
        res[3] = lat_swap(res[2], 1)
    parts = [part] + [code_part(res[k], w_dec) for k in others]
    early = width_sum(jnp.stack(parts[:-1]))
    code_sums = [early[k] for k in range(count - 1)] + [width_sum(parts[-1])]
    code_total = sum(jnp.sum(c.astype(f32), axis=0) for c in codes)
    squares = square_sums(after(w_dec, xs[1]))
    norms = jnp.sqrt(squares + 1e-06)
    sparsity = (sparsity_coef * row_scale * code_total / norms)[:, None] * w_dec.astype(f32)
    (grad_dec,) = dec_add(sparsity, codes, res)
    code_sums[-1], grad_dec = stage(code_sums[-1], grad_dec)
    grads, grad_benc, share = pre_grads(
        codes, code_sums, sparsity_coef * row_scale * norms, w_enc_t, res_grad
    )
    grad_enc = enc_end(centered, grads).T
    if line:
        near, far, cross = (lat_swap(share, k) for k in others)
        grad_bdec = (share + near) + (far + cross)
    else:
        grad_bdec, step = share, 1
        while step < count:
            grad_bdec = grad_bdec + lat_swap(grad_bdec, step)
            step *= 2
    return (grad_enc, grad_benc, grad_dec, grad_bdec[0])


def solution(mesh):
    placed = (
        P(("groups", "lat"), "width"),
        P(("groups", "lat"), "width"),
        P("width", "lat"),
        P("lat"),
        P("lat", "width"),
        P("width"),
    )
    return jax.shard_map(
        shards,
        mesh=mesh,
        in_specs=placed,
        out_specs=(
            P(("groups", "width"), "lat"),
            P(("groups", "lat")),
            P(("groups", "lat"), "width"),
            P(("groups", "width")),
        ),
        check_vma=False,
    )
```

```python
import jax
import jax.numpy as jnp
from jax import lax
from jax.experimental import pallas as pl
from jax.experimental.pallas import tpu as pltpu
from jax.sharding import PartitionSpec as P

sparsity_coef = 3.0
f32 = jnp.float32
bf16 = jnp.bfloat16


def swap(value, axis, distance):
    count = lax.axis_size(axis)
    return lax.ppermute(value, axis, [(i, i ^ distance) for i in range(count)])


def after(value, *earlier):
    return lax.optimization_barrier((value, *earlier))[0]


def stage(*values):
    return lax.optimization_barrier(values)


def width_sum(part):
    total, step = part.astype(f32), 1
    while step < lax.axis_size("width"):
        sent = lax.reduce_precision(total, 8, 7)
        total = sent + swap(sent.astype(bf16), "width", 2 * step - 1).astype(f32)
        step *= 2
    return total


def plain_sum(value, axis):
    step = 1
    while step < lax.axis_size(axis):
        value = value + swap(value, axis, step)
        step *= 2
    return value


def keeps_low():
    index, odd = lax.axis_index("width"), 0
    for bit in range((lax.axis_size("width") - 1).bit_length()):
        odd = odd ^ ((index >> bit) & 1)
    return odd == 0


def half_sum(part):
    rows, low = part.shape[0] // 2, keeps_low()
    keep = jnp.where(low, part[:rows], part[rows:])
    send = jnp.where(low, part[rows:], part[:rows])
    total, step = keep.astype(f32) + swap(send, "width", 1).astype(f32), 3
    while step < lax.axis_size("width") * 3 // 2:
        sent = lax.reduce_precision(total, 8, 7)
        total = sent + swap(sent.astype(bf16), "width", step).astype(f32)
        step *= 2
    return total


def join(kept):
    low, other = keeps_low(), swap(kept, "width", 1)
    return jnp.concatenate([jnp.where(low, kept, other), jnp.where(low, other, kept)])


def mm(a, b, contract):
    return lax.dot_general(a, b, ((contract[:1], contract[1:]), ((), ())), preferred_element_type=f32)


VMEM = pl.BlockSpec(memory_space=pltpu.VMEM)


def call(kernel, name, outs, *operands):
    return pl.pallas_call(
        kernel,
        out_shape=[jax.ShapeDtypeStruct(shape, kind) for shape, kind in outs],
        in_specs=[VMEM] * len(operands),
        out_specs=[VMEM] * len(outs),
        cost_estimate=pl.CostEstimate(flops=10**6, bytes_accessed=10**6, transcendentals=0),
        compiler_params=pltpu.CompilerParams(vmem_limit_bytes=24 * 2**20),
        name=name,
    )(*operands)


def part_of(x, b_dec, w_enc_t):
    def kernel(x_ref, b_ref, w_ref, centered_ref, part_ref):
        centered_ref[...] = (x_ref[...].astype(f32) - b_ref[...]).astype(bf16)
        part_ref[...] = mm(centered_ref[...], w_ref[...], (1, 1)).astype(bf16)

    outs = [(x.shape, bf16), ((x.shape[0], w_enc_t.shape[0]), bf16)]
    return call(kernel, "part_of", outs, x, b_dec[None], w_enc_t)


def recon_of(codes, w_dec, *sums):
    def kernel(c_ref, w_ref, *refs):
        value = mm(c_ref[...], w_ref[...], (1, 0))
        for ref in refs[:-1]:
            value = value + ref[...].astype(f32)
        refs[-1][...] = value.astype(bf16)

    outs = [((codes.shape[0], w_dec.shape[1]), bf16)]
    return call(kernel, "recon_of", outs, codes, w_dec, *sums)[0]


def res_of(scale, x, rest, b_dec, codes, w_dec, sums):
    def kernel(x_ref, r_ref, b_ref, c_ref, w_ref, *refs):
        value = r_ref[...].astype(f32) + b_ref[...] - x_ref[...].astype(f32)
        value = value + mm(c_ref[...], w_ref[...], (1, 0))
        for ref in refs[:-2]:
            value = value + ref[...].astype(f32)
        res_ref, part_ref = refs[-2:]
        res_ref[...] = (scale * value).astype(bf16)
        part_ref[...] = mm(res_ref[...], w_ref[...], (1, 1)).astype(bf16)

    outs = [(x.shape, bf16), (codes.shape, bf16)]
    return call(kernel, "res_of", outs, x, rest, b_dec[None], codes, w_dec, *sums)


def code_part(res, w_dec):
    def kernel(r_ref, w_ref, out):
        out[...] = mm(r_ref[...], w_ref[...], (1, 1)).astype(bf16)

    return call(kernel, "code_part", [((res.shape[0], w_dec.shape[0]), bf16)], res, w_dec)[0]


def dec_add(total, codes, res, *shares):
    count = len(res)

    def kernel(total_ref, *refs):
        value = sum(mm(refs[k][...], refs[count + k][...], (0, 0)) for k in range(count))
        refs[2 * count + len(shares)][...] = total_ref[...] + value
        if shares:
            refs[-1][...] = refs[2 * count][...] + refs[2 * count + 1][...]

    outs = [(total.shape, f32)] + [(s.shape, f32) for s in shares[:1]]
    return call(kernel, "dec_add", outs, total, *codes, *res, *shares)


def pre_grads(codes, sums, threshold, w_enc_t, res):
    count = len(codes)

    def kernel(n_ref, w_ref, res_ref, *refs):
        c, s = refs[:count], refs[count : 2 * count]
        out, bias, share = refs[2 * count :]
        total = 0.0
        for k in range(count):
            g = jnp.where(c[k][...].astype(f32) > 0, s[k][...] + n_ref[...], 0.0)
            out[k] = g.astype(bf16)
            total = total + jnp.sum(out[k].astype(f32), axis=0, keepdims=True)
        bias[...] = total
        high = total.astype(bf16)
        rest = total - high.astype(f32)
        mid = rest.astype(bf16)
        low = (rest - mid.astype(f32)).astype(bf16)
        row = lax.broadcasted_iota(jnp.int32, (8, total.shape[1]), 0)
        pieces = jnp.where(row == 0, high.astype(f32), jnp.where(row == 1, mid.astype(f32), 0.0))
        pieces = jnp.where(row == 2, low.astype(f32), pieces).astype(bf16)
        product = jnp.sum(mm(pieces, w_ref[...], (1, 0)), axis=0, keepdims=True)
        share[...] = jnp.sum(res_ref[...].astype(f32), axis=0, keepdims=True) - product

    lat, cols = w_enc_t.shape
    outs = [((count, *codes[0].shape), bf16), ((1, lat), f32), ((1, cols), f32)]
    grads, bias, share = call(
        kernel, "pre_grads", outs, threshold[None], w_enc_t, res, *codes, *sums
    )
    return grads, bias[0], share


def enc_end(centered, grads):
    count = len(centered)

    def kernel(g_ref, *refs):
        refs[-1][...] = sum(mm(g_ref[k], refs[k][...], (0, 0)) for k in range(count))

    outs = [((grads.shape[2], centered[0].shape[1]), f32)]
    return call(kernel, "enc_end", outs, grads, *centered)[0]


def square_sums(w_dec):
    dec_float = w_dec.astype(f32)
    value, step = jnp.sum(dec_float * dec_float, axis=1), 1
    while step < lax.axis_size("width"):
        value = value + swap(value, "width", 2 * step - 1)
        step *= 2
    return value


def shards(activations, rest_recon, w_enc, b_enc, w_dec, b_dec):
    count = lax.axis_size("lat")
    line = count == 4
    others = range(1, count)
    row_scale = float((activations.shape[0] * count) ** -0.5)
    w_enc_t = w_enc.T

    def lat_swap(block, distance):
        return swap(block, "lat", distance)

    xs = [activations] + [lat_swap(activations, k) if k != 2 or not line else None for k in others]
    centered, parts, codes = [None] * count, [None] * count, [None] * count

    def add_parts(blocks):
        for k in blocks:
            centered[k], parts[k] = part_of(xs[k], b_dec, w_enc_t)

    def add_codes(blocks, total):
        for i, k in enumerate(blocks):
            codes[k] = jnp.maximum(total[i] + b_enc, 0.0).astype(bf16)

    def sum_parts(blocks):
        return width_sum(jnp.stack([parts[k] for k in blocks]))

    add_parts([0])
    if line:
        xs[3], xs[1], centered[0], parts[0] = stage(xs[3], xs[1], centered[0], parts[0])
        xs[2] = lat_swap(xs[3], 1)
        add_parts([1, 3])
        kept = jnp.maximum(half_sum(parts[3]) + b_enc, 0.0).astype(bf16)
        codes[3] = join(kept)
        passed = lat_swap(recon_of(codes[3], w_dec), 1)
        add_parts([2])
        passed, total = stage(passed, sum_parts([0, 1, 2]))
        add_codes([0, 1, 2], total)
        onward = recon_of(codes[2], w_dec, passed)
        sums = [lat_swap(recon_of(after(codes[1], onward), w_dec), 1), lat_swap(onward, 2)]
    else:
        add_parts(others)
        add_codes(range(count), sum_parts(range(count)))
        sums = [lat_swap(recon_of(codes[k], w_dec), k) for k in others]
    res_grad, part = res_of(
        2.0 * row_scale, activations, rest_recon, b_dec, codes[0], w_dec, sums
    )

    res = [res_grad] + [lat_swap(res_grad, k) if k != 3 or not line else None for k in others]
    if line:
        res[2], res[1] = stage(res[2], res[1])
        res[3] = lat_swap(res[2], 1)
    parts = [part] + [code_part(res[k], w_dec) for k in others]
    early = width_sum(jnp.stack(parts[:-1]))
    code_sums = [early[k] for k in range(count - 1)] + [width_sum(parts[-1])]
    code_total = sum(jnp.sum(c.astype(f32), axis=0) for c in codes)
    squares = square_sums(after(w_dec, xs[1]))
    norms = jnp.sqrt(squares + 1e-06)
    sparsity = (sparsity_coef * row_scale * code_total / norms)[:, None] * w_dec.astype(f32)
    (grad_dec,) = dec_add(sparsity, codes, res)
    code_sums[-1], grad_dec = stage(code_sums[-1], grad_dec)
    grads, grad_benc, share = pre_grads(
        codes, code_sums, sparsity_coef * row_scale * norms, w_enc_t, res_grad
    )
    grad_enc = enc_end(centered, grads).T
    if line:
        near, far, cross = (lat_swap(share, k) for k in others)
        grad_bdec = (share + near) + (far + cross)
    else:
        grad_bdec, step = share, 1
        while step < count:
            grad_bdec = grad_bdec + lat_swap(grad_bdec, step)
            step *= 2
    return (grad_enc, grad_benc, grad_dec, grad_bdec[0])


def solution(mesh):
    placed = (
        P(("groups", "lat"), "width"),
        P(("groups", "lat"), "width"),
        P("width", "lat"),
        P("lat"),
        P("lat", "width"),
        P("width"),
    )
    return jax.shard_map(
        shards,
        mesh=mesh,
        in_specs=placed,
        out_specs=(
            P(("groups", "width"), "lat"),
            P(("groups", "lat")),
            P(("groups", "lat"), "width"),
            P(("groups", "width")),
        ),
        check_vma=False,
    )
```

```python
import jax
import jax.numpy as jnp
from jax import lax
from jax.experimental import pallas as pl
from jax.experimental.pallas import tpu as pltpu
from jax.sharding import PartitionSpec as P

sparsity_coef = 3.0
f32 = jnp.float32
bf16 = jnp.bfloat16


def swap(value, axis, distance):
    count = lax.axis_size(axis)
    return lax.ppermute(value, axis, [(i, i ^ distance) for i in range(count)])


def after(value, *earlier):
    return lax.optimization_barrier((value, *earlier))[0]


def stage(*values):
    return lax.optimization_barrier(values)


def width_sum(part):
    total, step = part.astype(f32), 1
    while step < lax.axis_size("width"):
        sent = lax.reduce_precision(total, 8, 7)
        total = sent + swap(sent.astype(bf16), "width", 2 * step - 1).astype(f32)
        step *= 2
    return total


def plain_sum(value, axis):
    step = 1
    while step < lax.axis_size(axis):
        value = value + swap(value, axis, step)
        step *= 2
    return value


def keeps_low():
    index, odd = lax.axis_index("width"), 0
    for bit in range((lax.axis_size("width") - 1).bit_length()):
        odd = odd ^ ((index >> bit) & 1)
    return odd == 0


def half_sum(part):
    rows, low = part.shape[0] // 2, keeps_low()
    keep = jnp.where(low, part[:rows], part[rows:])
    send = jnp.where(low, part[rows:], part[:rows])
    total, step = keep.astype(f32) + swap(send, "width", 1).astype(f32), 3
    while step < lax.axis_size("width") * 3 // 2:
        sent = lax.reduce_precision(total, 8, 7)
        total = sent + swap(sent.astype(bf16), "width", step).astype(f32)
        step *= 2
    return total


def join(kept):
    low, other = keeps_low(), swap(kept, "width", 1)
    return jnp.concatenate([jnp.where(low, kept, other), jnp.where(low, other, kept)])


def mm(a, b, contract):
    return lax.dot_general(a, b, ((contract[:1], contract[1:]), ((), ())), preferred_element_type=f32)


VMEM = pl.BlockSpec(memory_space=pltpu.VMEM)


def call(kernel, name, outs, *operands):
    return pl.pallas_call(
        kernel,
        out_shape=[jax.ShapeDtypeStruct(shape, kind) for shape, kind in outs],
        in_specs=[VMEM] * len(operands),
        out_specs=[VMEM] * len(outs),
        cost_estimate=pl.CostEstimate(flops=10**6, bytes_accessed=10**6, transcendentals=0),
        compiler_params=pltpu.CompilerParams(vmem_limit_bytes=24 * 2**20),
        name=name,
    )(*operands)


def part_of(x, b_dec, w_enc_t):
    def kernel(x_ref, b_ref, w_ref, centered_ref, part_ref):
        centered_ref[...] = (x_ref[...].astype(f32) - b_ref[...]).astype(bf16)
        part_ref[...] = mm(centered_ref[...], w_ref[...], (1, 1)).astype(bf16)

    outs = [(x.shape, bf16), ((x.shape[0], w_enc_t.shape[0]), bf16)]
    return call(kernel, "part_of", outs, x, b_dec[None], w_enc_t)


def recon_of(codes, w_dec, *sums):
    def kernel(c_ref, w_ref, *refs):
        value = mm(c_ref[...], w_ref[...], (1, 0))
        for ref in refs[:-1]:
            value = value + ref[...].astype(f32)
        refs[-1][...] = value.astype(bf16)

    outs = [((codes.shape[0], w_dec.shape[1]), bf16)]
    return call(kernel, "recon_of", outs, codes, w_dec, *sums)[0]


def res_of(scale, x, rest, b_dec, codes, w_dec, sums):
    def kernel(x_ref, r_ref, b_ref, c_ref, w_ref, *refs):
        value = r_ref[...].astype(f32) + b_ref[...] - x_ref[...].astype(f32)
        value = value + mm(c_ref[...], w_ref[...], (1, 0))
        for ref in refs[:-2]:
            value = value + ref[...].astype(f32)
        res_ref, part_ref = refs[-2:]
        res_ref[...] = (scale * value).astype(bf16)
        part_ref[...] = mm(res_ref[...], w_ref[...], (1, 1)).astype(bf16)

    outs = [(x.shape, bf16), (codes.shape, bf16)]
    return call(kernel, "res_of", outs, x, rest, b_dec[None], codes, w_dec, *sums)


def code_part(res, w_dec):
    def kernel(r_ref, w_ref, out):
        out[...] = mm(r_ref[...], w_ref[...], (1, 1)).astype(bf16)

    return call(kernel, "code_part", [((res.shape[0], w_dec.shape[0]), bf16)], res, w_dec)[0]


def dec_add(total, codes, res, *shares):
    count = len(res)

    def kernel(total_ref, *refs):
        value = sum(mm(refs[k][...], refs[count + k][...], (0, 0)) for k in range(count))
        refs[2 * count + len(shares)][...] = total_ref[...] + value
        if shares:
            refs[-1][...] = refs[2 * count][...] + refs[2 * count + 1][...]

    outs = [(total.shape, f32)] + [(s.shape, f32) for s in shares[:1]]
    return call(kernel, "dec_add", outs, total, *codes, *res, *shares)


def pre_grads(codes, sums, threshold, w_enc_t, res):
    count = len(codes)

    def kernel(n_ref, w_ref, res_ref, *refs):
        c, s = refs[:count], refs[count : 2 * count]
        out, bias, share = refs[2 * count :]
        total = 0.0
        for k in range(count):
            g = jnp.where(c[k][...].astype(f32) > 0, s[k][...] + n_ref[...], 0.0)
            out[k] = g.astype(bf16)
            total = total + jnp.sum(out[k].astype(f32), axis=0, keepdims=True)
        bias[...] = total
        high = total.astype(bf16)
        rest = total - high.astype(f32)
        mid = rest.astype(bf16)
        low = (rest - mid.astype(f32)).astype(bf16)
        row = lax.broadcasted_iota(jnp.int32, (8, total.shape[1]), 0)
        pieces = jnp.where(row == 0, high.astype(f32), jnp.where(row == 1, mid.astype(f32), 0.0))
        pieces = jnp.where(row == 2, low.astype(f32), pieces).astype(bf16)
        product = jnp.sum(mm(pieces, w_ref[...], (1, 0)), axis=0, keepdims=True)
        share[...] = jnp.sum(res_ref[...].astype(f32), axis=0, keepdims=True) - product

    lat, cols = w_enc_t.shape
    outs = [((count, *codes[0].shape), bf16), ((1, lat), f32), ((1, cols), f32)]
    grads, bias, share = call(
        kernel, "pre_grads", outs, threshold[None], w_enc_t, res, *codes, *sums
    )
    return grads, bias[0], share


def enc_end(centered, grads):
    count = len(centered)

    def kernel(g_ref, *refs):
        refs[-1][...] = sum(mm(g_ref[k], refs[k][...], (0, 0)) for k in range(count))

    outs = [((grads.shape[2], centered[0].shape[1]), f32)]
    return call(kernel, "enc_end", outs, grads, *centered)[0]


def square_sums(w_dec):
    dec_float = w_dec.astype(f32)
    value, step = jnp.sum(dec_float * dec_float, axis=1), 1
    while step < lax.axis_size("width"):
        value = value + swap(value, "width", 2 * step - 1)
        step *= 2
    return value


def shards(activations, rest_recon, w_enc, b_enc, w_dec, b_dec):
    count = lax.axis_size("lat")
    line = count == 4
    others = range(1, count)
    row_scale = float((activations.shape[0] * count) ** -0.5)
    w_enc_t = w_enc.T

    def lat_swap(block, distance):
        return swap(block, "lat", distance)

    xs = [activations] + [lat_swap(activations, k) if k != 2 or not line else None for k in others]
    centered, parts, codes = [None] * count, [None] * count, [None] * count

    def add_parts(blocks):
        for k in blocks:
            centered[k], parts[k] = part_of(xs[k], b_dec, w_enc_t)

    def add_codes(blocks, total):
        for i, k in enumerate(blocks):
            codes[k] = jnp.maximum(total[i] + b_enc, 0.0).astype(bf16)

    def sum_parts(blocks):
        return width_sum(jnp.stack([parts[k] for k in blocks]))

    add_parts([0])
    if line:
        xs[3], xs[1], centered[0], parts[0] = stage(xs[3], xs[1], centered[0], parts[0])
        xs[2] = lat_swap(xs[3], 1)
        add_parts([1, 3])
        kept = jnp.maximum(half_sum(parts[3]) + b_enc, 0.0).astype(bf16)
        codes[3] = join(kept)
        passed = lat_swap(recon_of(codes[3], w_dec), 1)
        add_parts([2])
        passed, total = stage(passed, sum_parts([0, 1, 2]))
        add_codes([0, 1, 2], total)
        onward = recon_of(codes[2], w_dec, passed)
        sums = [lat_swap(recon_of(after(codes[1], onward), w_dec), 1), lat_swap(onward, 2)]
    else:
        add_parts(others)
        add_codes(range(count), sum_parts(range(count)))
        sums = [lat_swap(recon_of(codes[k], w_dec), k) for k in others]
    res_grad, part = res_of(
        2.0 * row_scale, activations, rest_recon, b_dec, codes[0], w_dec, sums
    )

    res = [res_grad] + [lat_swap(res_grad, k) if k != 3 or not line else None for k in others]
    if line:
        res[2], res[1] = stage(res[2], res[1])
        res[3] = lat_swap(res[2], 1)
    parts = [part] + [code_part(res[k], w_dec) for k in others]
    early = width_sum(jnp.stack(parts[:-1]))
    code_sums = [early[k] for k in range(count - 1)] + [width_sum(parts[-1])]
    code_total = sum(jnp.sum(c.astype(f32), axis=0) for c in codes)
    squares = square_sums(after(w_dec, xs[1]))
    norms = jnp.sqrt(squares + 1e-06)
    sparsity = (sparsity_coef * row_scale * code_total / norms)[:, None] * w_dec.astype(f32)
    (grad_dec,) = dec_add(sparsity, codes, res)
    code_sums[-1], grad_dec = stage(code_sums[-1], grad_dec)
    grads, grad_benc, share = pre_grads(
        codes, code_sums, sparsity_coef * row_scale * norms, w_enc_t, res_grad
    )
    grad_enc = enc_end(centered, grads).T
    if line:
        cross, far, near = stage(*(lat_swap(share, k) for k in (3, 2, 1)))
        grad_bdec = (share + near) + (far + cross)
    else:
        grad_bdec, step = share, 1
        while step < count:
            grad_bdec = grad_bdec + lat_swap(grad_bdec, step)
            step *= 2
    return (grad_enc, grad_benc, grad_dec, grad_bdec[0])


def solution(mesh):
    placed = (
        P(("groups", "lat"), "width"),
        P(("groups", "lat"), "width"),
        P("width", "lat"),
        P("lat"),
        P("lat", "width"),
        P("width"),
    )
    return jax.shard_map(
        shards,
        mesh=mesh,
        in_specs=placed,
        out_specs=(
            P(("groups", "width"), "lat"),
            P(("groups", "lat")),
            P(("groups", "lat"), "width"),
            P(("groups", "width")),
        ),
        check_vma=False,
    )
```

```python
import jax
import jax.numpy as jnp
from jax import lax
from jax.experimental import pallas as pl
from jax.experimental.pallas import tpu as pltpu
from jax.sharding import PartitionSpec as P

sparsity_coef = 3.0
f32 = jnp.float32
bf16 = jnp.bfloat16


def swap(value, axis, distance):
    count = lax.axis_size(axis)
    return lax.ppermute(value, axis, [(i, i ^ distance) for i in range(count)])


def after(value, *earlier):
    return lax.optimization_barrier((value, *earlier))[0]


def stage(*values):
    return lax.optimization_barrier(values)


def width_sum(part):
    total, step = part.astype(f32), 1
    while step < lax.axis_size("width"):
        sent = lax.reduce_precision(total, 8, 7)
        total = sent + swap(sent.astype(bf16), "width", 2 * step - 1).astype(f32)
        step *= 2
    return total


def plain_sum(value, axis):
    step = 1
    while step < lax.axis_size(axis):
        value = value + swap(value, axis, step)
        step *= 2
    return value


def keeps_low():
    index, odd = lax.axis_index("width"), 0
    for bit in range((lax.axis_size("width") - 1).bit_length()):
        odd = odd ^ ((index >> bit) & 1)
    return odd == 0


def half_sum(part):
    rows, low = part.shape[0] // 2, keeps_low()
    keep = jnp.where(low, part[:rows], part[rows:])
    send = jnp.where(low, part[rows:], part[:rows])
    total, step = keep.astype(f32) + swap(send, "width", 1).astype(f32), 3
    while step < lax.axis_size("width") * 3 // 2:
        sent = lax.reduce_precision(total, 8, 7)
        total = sent + swap(sent.astype(bf16), "width", step).astype(f32)
        step *= 2
    return total


def join(kept):
    low, other = keeps_low(), swap(kept, "width", 1)
    return jnp.concatenate([jnp.where(low, kept, other), jnp.where(low, other, kept)])


def mm(a, b, contract):
    return lax.dot_general(a, b, ((contract[:1], contract[1:]), ((), ())), preferred_element_type=f32)


VMEM = pl.BlockSpec(memory_space=pltpu.VMEM)


def call(kernel, name, outs, *operands):
    return pl.pallas_call(
        kernel,
        out_shape=[jax.ShapeDtypeStruct(shape, kind) for shape, kind in outs],
        in_specs=[VMEM] * len(operands),
        out_specs=[VMEM] * len(outs),
        cost_estimate=pl.CostEstimate(flops=10**6, bytes_accessed=10**6, transcendentals=0),
        compiler_params=pltpu.CompilerParams(vmem_limit_bytes=24 * 2**20),
        name=name,
    )(*operands)


def part_of(x, b_dec, w_enc_t):
    def kernel(x_ref, b_ref, w_ref, centered_ref, part_ref):
        centered_ref[...] = (x_ref[...].astype(f32) - b_ref[...]).astype(bf16)
        part_ref[...] = mm(centered_ref[...], w_ref[...], (1, 1)).astype(bf16)

    outs = [(x.shape, bf16), ((x.shape[0], w_enc_t.shape[0]), bf16)]
    return call(kernel, "part_of", outs, x, b_dec[None], w_enc_t)


def recon_of(codes, w_dec, *sums):
    def kernel(c_ref, w_ref, *refs):
        value = mm(c_ref[...], w_ref[...], (1, 0))
        for ref in refs[:-1]:
            value = value + ref[...].astype(f32)
        refs[-1][...] = value.astype(bf16)

    outs = [((codes.shape[0], w_dec.shape[1]), bf16)]
    return call(kernel, "recon_of", outs, codes, w_dec, *sums)[0]


def res_of(scale, x, rest, b_dec, codes, w_dec, sums):
    def kernel(x_ref, r_ref, b_ref, c_ref, w_ref, *refs):
        value = r_ref[...].astype(f32) + b_ref[...] - x_ref[...].astype(f32)
        value = value + mm(c_ref[...], w_ref[...], (1, 0))
        for ref in refs[:-2]:
            value = value + ref[...].astype(f32)
        res_ref, part_ref = refs[-2:]
        res_ref[...] = (scale * value).astype(bf16)
        part_ref[...] = mm(res_ref[...], w_ref[...], (1, 1)).astype(bf16)

    outs = [(x.shape, bf16), (codes.shape, bf16)]
    return call(kernel, "res_of", outs, x, rest, b_dec[None], codes, w_dec, *sums)


def code_part(res, w_dec):
    def kernel(r_ref, w_ref, out):
        out[...] = mm(r_ref[...], w_ref[...], (1, 1)).astype(bf16)

    return call(kernel, "code_part", [((res.shape[0], w_dec.shape[0]), bf16)], res, w_dec)[0]


def dec_add(total, codes, res, *shares):
    count = len(res)

    def kernel(total_ref, *refs):
        value = sum(mm(refs[k][...], refs[count + k][...], (0, 0)) for k in range(count))
        refs[2 * count + len(shares)][...] = total_ref[...] + value
        if shares:
            refs[-1][...] = refs[2 * count][...] + refs[2 * count + 1][...]

    outs = [(total.shape, f32)] + [(s.shape, f32) for s in shares[:1]]
    return call(kernel, "dec_add", outs, total, *codes, *res, *shares)


def pre_grads(codes, sums, threshold, w_enc_t, res_sum):
    count = len(codes)

    def kernel(n_ref, w_ref, res_ref, *refs):
        c, s = refs[:count], refs[count : 2 * count]
        out, bias, share = refs[2 * count :]
        total = 0.0
        for k in range(count):
            g = jnp.where(c[k][...].astype(f32) > 0, s[k][...] + n_ref[...], 0.0)
            out[k] = g.astype(bf16)
            total = total + jnp.sum(out[k].astype(f32), axis=0, keepdims=True)
        bias[...] = total
        high = total.astype(bf16)
        rest = total - high.astype(f32)
        mid = rest.astype(bf16)
        low = (rest - mid.astype(f32)).astype(bf16)
        row = lax.broadcasted_iota(jnp.int32, (8, total.shape[1]), 0)
        pieces = jnp.where(row == 0, high.astype(f32), jnp.where(row == 1, mid.astype(f32), 0.0))
        pieces = jnp.where(row == 2, low.astype(f32), pieces).astype(bf16)
        product = jnp.sum(mm(pieces, w_ref[...], (1, 0)), axis=0, keepdims=True)
        share[...] = res_ref[...] - product

    lat, cols = w_enc_t.shape
    outs = [((count, *codes[0].shape), bf16), ((1, lat), f32), ((1, cols), f32)]
    grads, bias, share = call(
        kernel, "pre_grads", outs, threshold[None], w_enc_t, res_sum, *codes, *sums
    )
    return grads, bias[0], share


def enc_end(centered, grads):
    count = len(centered)

    def kernel(g_ref, *refs):
        refs[-1][...] = sum(mm(g_ref[k], refs[k][...], (0, 0)) for k in range(count))

    outs = [((grads.shape[2], centered[0].shape[1]), f32)]
    return call(kernel, "enc_end", outs, grads, *centered)[0]


def square_sums(w_dec):
    dec_float = w_dec.astype(f32)
    value, step = jnp.sum(dec_float * dec_float, axis=1), 1
    while step < lax.axis_size("width"):
        value = value + swap(value, "width", 2 * step - 1)
        step *= 2
    return value


def shards(activations, rest_recon, w_enc, b_enc, w_dec, b_dec):
    count = lax.axis_size("lat")
    line = count == 4
    others = range(1, count)
    row_scale = float((activations.shape[0] * count) ** -0.5)
    w_enc_t = w_enc.T

    def lat_swap(block, distance):
        return swap(block, "lat", distance)

    xs = [activations] + [lat_swap(activations, k) if k != 2 or not line else None for k in others]
    centered, parts, codes = [None] * count, [None] * count, [None] * count

    def add_parts(blocks):
        for k in blocks:
            centered[k], parts[k] = part_of(xs[k], b_dec, w_enc_t)

    def add_codes(blocks, total):
        for i, k in enumerate(blocks):
            codes[k] = jnp.maximum(total[i] + b_enc, 0.0).astype(bf16)

    def sum_parts(blocks):
        return width_sum(jnp.stack([parts[k] for k in blocks]))

    add_parts([0])
    if line:
        xs[3], xs[1], centered[0], parts[0] = stage(xs[3], xs[1], centered[0], parts[0])
        xs[2] = lat_swap(xs[3], 1)
        add_parts([1, 3])
        kept = jnp.maximum(half_sum(parts[3]) + b_enc, 0.0).astype(bf16)
        codes[3] = join(kept)
        passed = lat_swap(recon_of(codes[3], w_dec), 1)
        add_parts([2])
        passed, total = stage(passed, sum_parts([0, 1, 2]))
        add_codes([0, 1, 2], total)
        onward = recon_of(codes[2], w_dec, passed)
        sums = [lat_swap(recon_of(after(codes[1], onward), w_dec), 1), lat_swap(onward, 2)]
    else:
        add_parts(others)
        add_codes(range(count), sum_parts(range(count)))
        sums = [lat_swap(recon_of(codes[k], w_dec), k) for k in others]
    res_grad, part = res_of(
        2.0 * row_scale, activations, rest_recon, b_dec, codes[0], w_dec, sums
    )

    res = [res_grad] + [lat_swap(res_grad, k) if k != 3 or not line else None for k in others]
    if line:
        res[2], res[1] = stage(res[2], res[1])
        res[3] = lat_swap(res[2], 1)
    parts = [part] + [code_part(res[k], w_dec) for k in others]
    early = width_sum(jnp.stack(parts[:-1]))
    code_sums = [early[k] for k in range(count - 1)] + [width_sum(parts[-1])]
    code_total = sum(jnp.sum(c.astype(f32), axis=0) for c in codes)
    squares = square_sums(after(w_dec, xs[1]))
    norms = jnp.sqrt(squares + 1e-06)
    sparsity = (sparsity_coef * row_scale * code_total / norms)[:, None] * w_dec.astype(f32)
    (grad_dec,) = dec_add(sparsity, codes, res)
    res_sum = jnp.sum(res_grad.astype(f32), axis=0, keepdims=True)
    code_sums[-1], grad_dec, res_sum = stage(code_sums[-1], grad_dec, res_sum)
    grads, grad_benc, share = pre_grads(
        codes, code_sums, sparsity_coef * row_scale * norms, w_enc_t, res_sum
    )
    grad_enc = enc_end(centered, grads).T
    if line:
        cross, far, near = stage(*(lat_swap(share, k) for k in (3, 2, 1)))
        grad_bdec = (share + near) + (far + cross)
    else:
        grad_bdec, step = share, 1
        while step < count:
            grad_bdec = grad_bdec + lat_swap(grad_bdec, step)
            step *= 2
    return (grad_enc, grad_benc, grad_dec, grad_bdec[0])


def solution(mesh):
    placed = (
        P(("groups", "lat"), "width"),
        P(("groups", "lat"), "width"),
        P("width", "lat"),
        P("lat"),
        P("lat", "width"),
        P("width"),
    )
    return jax.shard_map(
        shards,
        mesh=mesh,
        in_specs=placed,
        out_specs=(
            P(("groups", "width"), "lat"),
            P(("groups", "lat")),
            P(("groups", "lat"), "width"),
            P(("groups", "width")),
        ),
        check_vma=False,
    )
```
